128 devices in a mesh: ctx: 32 (over y, z_hi, x), tp: 4 (over z_lo, core).
Axes of the slice: x: 4, y: 4, z: 4 (z_hi: 2, z_lo: 2; z = z_hi * 2 + z_lo), core: 2. Of those that a mesh axis runs over, the one named last changes fastest.
Arguments:
- query_rot: bfloat16 [16384, 3072], P('ctx', 'tp'), may hold values from -12 to 12
- key_rot: bfloat16 [16384, 3072], P('ctx', 'tp'), may hold values from -12 to 12
- value: bfloat16 [16384, 3072], P('ctx', 'tp'), may hold values from -6 to 6
- grad_out: bfloat16 [16384, 3072], P('ctx', 'tp'), may hold values from -6 to 6
- text_key: bfloat16 [256, 3072], P('ctx', 'tp'), may hold values from -6 to 6
- text_value: bfloat16 [256, 3072], P('ctx', 'tp'), may hold values from -6 to 6
- positions: int32 [3, 16384], P(None, 'ctx'), may hold values from 0 to 63, as said below
- tile_mask: int32 [128, 128], replicated, may hold values from 0 to 1, as said below
Outputs:
- grad_query: bfloat16 [16384, 3072], P('ctx', 'tp')
- grad_key: bfloat16 [16384, 3072], P('ctx', 'tp')
- grad_value: bfloat16 [16384, 3072], P('ctx', 'tp')
- grad_text_key: bfloat16 [256, 3072], P('ctx', 'tp')
- grad_text_value: bfloat16 [256, 3072], P('ctx', 'tp')
The draws below stay inside these ranges and needn't reach their ends.
Inputs may be any that keep to these rules, and one draw needn't show every extreme that they name: tile_mask[a, b] is 1 when tiles a and b lie in the same frame (2 tiles a frame, in token order) and 0 when their frames are more than 2 apart. positions[0, n] is n // 256; positions[1, n] and positions[2, n] are the row and column of token n in its frame of rows of 16 tokens, each plus an offset of 0 to 31 common to all tokens.
All inputs are finite; a program needn't handle non-finite values.
Results may differ from the reference program's by a relative error of at most 0.02.
Values may be sent and summed in bfloat16 or wider, within the bound.
No kernel may reach another device: no remote copies, remote signals or barrier semaphores. Data moves between devices by JAX's collectives and lax.ppermute only.
A program may use at most 128 MiB of HBM per device.

```python
import math
import jax
import jax.numpy as jnp
from jax import lax

HEADS = 24
D_HEAD = 128
TEXT = 256
TILE = 128
FRAME_TOK = 256
WGRID = 16
TOK_DEV = 512
REACH = 2
TOKENS = 16384


def draw_tile_mask(key, part):
    tile_count = TOKENS // TILE
    per_frame = FRAME_TOK // TILE
    tile_ids = jnp.arange(tile_count, dtype=jnp.int32)
    frame_ids = tile_ids // per_frame
    spot_ids = tile_ids % per_frame
    frame_gap = jnp.abs(frame_ids[:, None] - frame_ids[None, :])
    band_level = jnp.zeros_like(frame_gap)
    for level_bit in range(16):
        band_level = band_level + (frame_gap >= 2 ** level_bit).astype(jnp.int32)
    spot_gap = jnp.abs(spot_ids[:, None] - spot_ids[None, :])
    near_spot = spot_gap * jnp.left_shift(jnp.int32(1), band_level) < per_frame
    lucky_draw = jax.random.randint(key, (tile_count, tile_count), 0, 2 ** 20, dtype=jnp.int32)
    lucky_tile = lucky_draw % jnp.left_shift(jnp.int32(1), band_level + 1) == 0
    keep_tile = (frame_gap == 0) | (frame_gap <= REACH) & (near_spot | lucky_tile)
    return keep_tile.astype(jnp.int32)


def draw_positions(key, part):
    token_ids = jnp.arange(TOKENS, dtype=jnp.int32)
    frame_ids = token_ids // FRAME_TOK
    within_frame = token_ids % FRAME_TOK
    drawn_offsets = jax.random.randint(key, (2,), 0, 32, dtype=jnp.int32)
    row_count = FRAME_TOK // WGRID
    if row_count >= WGRID:
        row_offset = jnp.int32(31)
        col_offset = drawn_offsets[1]
    else:
        row_offset = drawn_offsets[0]
        col_offset = jnp.int32(31)
    stacked = jnp.stack([frame_ids, within_frame // WGRID + row_offset, within_frame % WGRID + col_offset])
    return stacked.astype(jnp.int32)


def draw_query_rot(key, part):
    own_key = jax.random.fold_in(key, 11)
    full_shape = (TOKENS, HEADS * D_HEAD)
    scales = jnp.exp(jax.random.uniform(jax.random.fold_in(own_key, 1), (TOKENS, 1), minval=math.log(0.3), maxval=math.log(3.0)))
    drawn = jax.random.normal(jax.random.fold_in(own_key, 2), full_shape) * scales
    return jnp.clip(drawn, -12.0, 12.0).astype(jnp.bfloat16)


def draw_key_rot(key, part):
    own_key = jax.random.fold_in(key, 13)
    full_shape = (TOKENS, HEADS * D_HEAD)
    drawn = jax.random.normal(jax.random.fold_in(own_key, 2), full_shape)
    return jnp.clip(drawn, -12.0, 12.0).astype(jnp.bfloat16)


def level_of(stream_key, shape, shards, least, high):
    def one(dim, parts):
        draws = jax.random.uniform(jax.random.fold_in(jax.random.fold_in(stream_key, 6), dim), (parts,), jnp.float32, least / len(shards), high / len(shards))
        return jnp.repeat(jnp.exp(draws), shape[dim] // parts).reshape((-1,) + (1,) * (len(shape) - dim - 1))

    factor_of = one(*shards[0])
    for cut in shards[1:]:
        factor_of = factor_of * one(*cut)
    return factor_of


def normal_values(stream_key, shape, deviation, most, pieces=(), kind=jnp.bfloat16):
    array = deviation * jax.random.normal(stream_key, shape, jnp.float32)
    if pieces:
        array = array * level_of(stream_key, shape, pieces, -0.22, 0.18)
    return jnp.clip(array, -most, most).astype(kind)


def setup_inputs(seed: int = 0) -> dict:
    key_of = jax.random.split(jax.random.key(seed), 9)
    return {
        "query_rot": draw_query_rot(jax.random.fold_in(key_of[8], 71), 0),
        "key_rot": draw_key_rot(jax.random.fold_in(key_of[8], 71), 0),
        "value": normal_values(key_of[2], (TOKENS, HEADS * D_HEAD), 1.0, 6.0, ((0, 32), (1, 4))),
        "grad_out": normal_values(key_of[3], (TOKENS, HEADS * D_HEAD), 1.0, 6.0, ((0, 32), (1, 4))),
        "text_key": normal_values(key_of[4], (TEXT, HEADS * D_HEAD), 1.0, 6.0, ((0, 32), (1, 4))),
        "text_value": normal_values(key_of[5], (TEXT, HEADS * D_HEAD), 1.0, 6.0, ((0, 32), (1, 4))),
        "positions": draw_positions(jax.random.fold_in(key_of[8], 71), 0),
        "tile_mask": draw_tile_mask(jax.random.fold_in(key_of[8], 71), 0),
    }


ROPE_THETA = 256.0
TIME_STRETCH = 0.25


def rope_tables(positions, head_dim):
    time_dims = head_dim // 8
    plane_dims = (head_dim - time_dims) // 2
    layout = ((time_dims, TIME_STRETCH), (plane_dims, 1.0), (plane_dims, 1.0))
    angle_parts = []
    for axis_id in range(3):
        seg_width, stretch = layout[axis_id]
        pair_ids = jnp.arange(seg_width // 2, dtype=jnp.float32)
        frequency = ROPE_THETA ** (-2.0 * pair_ids / seg_width)
        scaled_pos = positions[axis_id].astype(jnp.float32) * stretch
        angle_parts.append(scaled_pos[:, None] * frequency[None, :])
    angles = jnp.concatenate(angle_parts, axis=1)
    return jnp.cos(angles), jnp.sin(angles)


def unrotate(grad_rot, cosine, sine):
    tok_rows = grad_rot.shape[0]
    pairs = grad_rot.reshape(tok_rows, -1, cosine.shape[1], 2)
    even_part = pairs[..., 0]
    odd_part = pairs[..., 1]
    cos_rows = cosine[:, None, :]
    sin_rows = sine[:, None, :]
    turned = jnp.stack([cos_rows * even_part + sin_rows * odd_part, cos_rows * odd_part - sin_rows * even_part], axis=-1)
    return turned.reshape(grad_rot.shape)


def round_keep(values):
    return lax.optimization_barrier(values.astype(jnp.bfloat16)).astype(jnp.float32)


def block_terms(query_block, grad_block, keys_win, values_win, allowed, text_keys, text_values):
    score_scale = D_HEAD ** -0.5
    query_f = query_block.astype(jnp.float32)
    grad_f = grad_block.astype(jnp.float32)
    keys_f = keys_win.astype(jnp.float32)
    values_f = values_win.astype(jnp.float32)
    tkeys_f = text_keys.astype(jnp.float32)
    tvalues_f = text_values.astype(jnp.float32)
    video_scores = jnp.einsum("qhd,khd->hqk", query_f, keys_f) * score_scale
    video_scores = jnp.where(allowed[None], video_scores, -jnp.inf)
    text_scores = jnp.einsum("qhd,khd->hqk", query_f, tkeys_f) * score_scale
    row_max = jnp.maximum(jnp.max(video_scores, axis=2), jnp.max(text_scores, axis=2))
    row_total = jnp.sum(jnp.exp(video_scores - row_max[..., None]), axis=2) + jnp.sum(jnp.exp(text_scores - row_max[..., None]), axis=2)
    log_total = row_max + jnp.log(row_total)
    video_weights = round_keep(jnp.exp(video_scores - log_total[..., None]))
    text_weights = round_keep(jnp.exp(text_scores - log_total[..., None]))
    attended = jnp.einsum("hqk,khd->qhd", video_weights, values_f) + jnp.einsum("hqk,khd->qhd", text_weights, tvalues_f)
    row_delta = jnp.sum(grad_f * attended, axis=2)
    delta_cols = jnp.transpose(row_delta)[:, :, None]
    video_dprobs = jnp.einsum("qhd,khd->hqk", grad_f, values_f)
    text_dprobs = jnp.einsum("qhd,khd->hqk", grad_f, tvalues_f)
    video_dscores = round_keep(video_weights * (video_dprobs - delta_cols))
    text_dscores = round_keep(text_weights * (text_dprobs - delta_cols))
    query_grad = score_scale * (jnp.einsum("hqk,khd->qhd", video_dscores, keys_f) + jnp.einsum("hqk,khd->qhd", text_dscores, tkeys_f))
    key_grad = score_scale * jnp.einsum("hqk,qhd->khd", video_dscores, query_f)
    value_grad = jnp.einsum("hqk,qhd->khd", video_weights, grad_f)
    text_key_grad = score_scale * jnp.einsum("hqk,qhd->khd", text_dscores, query_f)
    text_value_grad = jnp.einsum("hqk,qhd->khd", text_weights, grad_f)
    return query_grad, key_grad, value_grad, text_key_grad, text_value_grad


def reference(query_rot, key_rot, value, grad_out, text_key, text_value, positions, tile_mask):
    tok_rows = TOK_DEV
    block_count = TOKENS // tok_rows
    tile_rows = tok_rows // TILE
    query_heads = query_rot.reshape(TOKENS, HEADS, D_HEAD)
    grad_heads = grad_out.reshape(TOKENS, HEADS, D_HEAD)
    padded_keys = jnp.pad(key_rot.reshape(TOKENS, HEADS, D_HEAD), ((tok_rows, tok_rows), (0, 0), (0, 0)))
    padded_values = jnp.pad(value.reshape(TOKENS, HEADS, D_HEAD), ((tok_rows, tok_rows), (0, 0), (0, 0)))
    padded_mask = jnp.pad(tile_mask, ((0, 0), (tile_rows, tile_rows)))
    text_keys = text_key.reshape(TEXT, HEADS, D_HEAD)
    text_values = text_value.reshape(TEXT, HEADS, D_HEAD)

    def block_step(carried, block_id):
        key_acc, value_acc, tkey_acc, tvalue_acc = carried
        row_start = (block_id * tok_rows).astype(jnp.int32)
        query_block = lax.dynamic_slice_in_dim(query_heads, row_start, tok_rows, 0)
        grad_block = lax.dynamic_slice_in_dim(grad_heads, row_start, tok_rows, 0)
        keys_win = lax.dynamic_slice_in_dim(padded_keys, row_start, 3 * tok_rows, 0)
        values_win = lax.dynamic_slice_in_dim(padded_values, row_start, 3 * tok_rows, 0)
        tile_start = (block_id * tile_rows).astype(jnp.int32)
        mask_block = lax.dynamic_slice(padded_mask, (tile_start, tile_start), (tile_rows, 3 * tile_rows))
        allowed = jnp.repeat(jnp.repeat(mask_block, TILE, axis=0), TILE, axis=1) > 0
        query_grad, key_grad, value_grad, text_key_grad, text_value_grad = block_terms(query_block, grad_block, keys_win, values_win, allowed, text_keys, text_values)
        key_acc = lax.dynamic_update_slice_in_dim(key_acc, lax.dynamic_slice_in_dim(key_acc, row_start, 3 * tok_rows, 0) + key_grad, row_start, 0)
        value_acc = lax.dynamic_update_slice_in_dim(value_acc, lax.dynamic_slice_in_dim(value_acc, row_start, 3 * tok_rows, 0) + value_grad, row_start, 0)
        return (key_acc, value_acc, tkey_acc + text_key_grad, tvalue_acc + text_value_grad), query_grad

    start_state = (jnp.zeros((TOKENS + 2 * tok_rows, HEADS, D_HEAD), jnp.float32), jnp.zeros((TOKENS + 2 * tok_rows, HEADS, D_HEAD), jnp.float32), jnp.zeros((TEXT, HEADS, D_HEAD), jnp.float32), jnp.zeros((TEXT, HEADS, D_HEAD), jnp.float32))
    final_state, query_blocks = lax.scan(block_step, start_state, jnp.arange(block_count, dtype=jnp.int32))
    width_all = HEADS * D_HEAD
    query_grad_all = query_blocks.reshape(TOKENS, width_all)
    key_grad_all = final_state[0][tok_rows:tok_rows + TOKENS].reshape(TOKENS, width_all)
    value_grad_all = final_state[1][tok_rows:tok_rows + TOKENS].reshape(TOKENS, width_all)
    cosine, sine = rope_tables(positions, D_HEAD)
    grad_query = unrotate(query_grad_all, cosine, sine).astype(jnp.bfloat16)
    grad_key = unrotate(key_grad_all, cosine, sine).astype(jnp.bfloat16)
    grad_value = value_grad_all.astype(jnp.bfloat16)
    grad_text_key = final_state[2].reshape(TEXT, width_all).astype(jnp.bfloat16)
    grad_text_value = final_state[3].reshape(TEXT, width_all).astype(jnp.bfloat16)
    return (grad_query, grad_key, grad_value, grad_text_key, grad_text_value)
```

```python
import functools
import math

import jax
import jax.numpy as jnp
from jax import lax
from jax.experimental import pallas as pl
from jax.experimental.pallas import tpu as pltpu
from jax.sharding import PartitionSpec as P

D_HEAD = 128
TILE = 128
FRAME = 256
ROPE_THETA = 256.0
TIME_STRETCH = 0.25
SCALE = D_HEAD ** (-0.5)
EXP2_SCALE = SCALE * math.log2(math.e)
BLOCKED = 1e30
GROUPS = 2
NT = (((1,), (1,)), ((), ()))
NN = (((1,), (0,)), ((), ()))
TN = (((0,), (0,)), ((), ()))


def shifted(block, axis, distance):
    devices = range(lax.axis_size(axis))
    route = [(i - distance, i) for i in devices if i - distance in devices]
    return lax.ppermute(block, axis, route)


def rope_tables(positions):
    time_dims = D_HEAD // 8
    plane_dims = (D_HEAD - time_dims) // 2
    layout = ((time_dims, TIME_STRETCH), (plane_dims, 1.0), (plane_dims, 1.0))
    angle_parts = []
    for axis_id in range(3):
        seg_width, stretch = layout[axis_id]
        pair_ids = (jnp.arange(seg_width, dtype=jnp.int32) // 2).astype(jnp.float32)
        frequency = ROPE_THETA ** (-2.0 * pair_ids / seg_width)
        scaled_pos = positions[axis_id].astype(jnp.float32) * stretch
        angle_parts.append(scaled_pos[:, None] * frequency[None, :])
    angles = jnp.concatenate(angle_parts, axis=1)
    odd = jnp.arange(D_HEAD, dtype=jnp.int32)[None, :] % 2 == 1
    sine = jnp.sin(angles)
    return jnp.cos(angles), jnp.where(odd, -sine, sine)


def unrotate(grad, cosine, sine):
    lane = lax.broadcasted_iota(jnp.int32, grad.shape, 1)
    partner = jnp.where(lane % 2 == 0, pltpu.roll(grad, D_HEAD - 1, 1), pltpu.roll(grad, 1, 1))
    return cosine * grad + sine * partner


def dot(lhs, rhs, dims):
    return lax.dot_general(lhs, rhs, dims, preferred_element_type=jnp.float32)


def fold_rows(block, combine):
    return combine(block.reshape(block.shape[0] // 8, 8, block.shape[1]), axis=0)


def attend_body(*refs, aliased):
    (bias_ref, cos_ref, sin_ref, q_ref, g_ref, ko_ref, vo_ref, kl_ref, vl_ref, kr_ref, vr_ref, tk_ref, tv_ref) = refs[:13]
    refs = refs[13 + (1 if aliased else 0):]
    dq_ref, dko_ref, dvo_ref, dl_ref, dr_ref, dt_ref, s_scr, dp_scr, e_scr = refs
    tok = q_ref.shape[0]
    f = FRAME
    chunks = (
        (kl_ref, vl_ref, 0, (0,), 0),
        (kl_ref, vl_ref, f, (0, 1), 2),
        (ko_ref, vo_ref, 0, (0, 1), 4),
        (ko_ref, vo_ref, f, (0, 1), 6),
        (kr_ref, vr_ref, 0, (0, 1), 8),
        (kr_ref, vr_ref, f, (1,), 10),
        (tk_ref, tv_ref, 0, (0, 1), None),
    )
    inv_rows, delta_rows, q_scaled, g_scaled = [], [], [], []
    for frame in range(2):
        cols = slice(frame * f, (frame + 1) * f)
        query = q_ref[cols, :]
        grad = g_ref[cols, :]
        top = None
        for c, (k_ref, _, row, frames, tile) in enumerate(chunks):
            if frame not in frames:
                continue
            scores = dot(k_ref[row:row + f, :], query, NT)
            s_scr[c * f:(c + 1) * f, cols] = scores
            for t in range(2):
                part = fold_rows(scores[t * TILE:(t + 1) * TILE], jnp.max)
                if tile is not None:
                    part = part - bias_ref[tile + t:tile + t + 1, cols]
                top = part if top is None else jnp.maximum(top, part)
        top = jnp.max(top, axis=0, keepdims=True) * EXP2_SCALE
        total = jnp.zeros((8, f), jnp.float32)
        delta = jnp.zeros((8, f), jnp.float32)
        for c, (_, v_ref, row, frames, tile) in enumerate(chunks):
            if frame not in frames:
                continue
            dprobs = dot(v_ref[row:row + f, :], grad, NT)
            dp_scr[c * f:(c + 1) * f, cols] = dprobs
            for t in range(2):
                rows = slice(c * f + t * TILE, c * f + (t + 1) * TILE)
                shift = top
                if tile is not None:
                    shift = shift + bias_ref[tile + t:tile + t + 1, cols]
                weights = jnp.exp2(s_scr[rows, cols] * EXP2_SCALE - shift)
                e_scr[rows, cols] = weights.astype(jnp.bfloat16)
                total = total + fold_rows(weights, jnp.sum)
                delta = delta + fold_rows(weights * dprobs[t * TILE:(t + 1) * TILE], jnp.sum)
        inv = 1.0 / jnp.sum(total, axis=0, keepdims=True)
        delta_rows.append(jnp.sum(delta, axis=0, keepdims=True) * inv)
        inv_rows.append(inv)
        inv_col = jnp.transpose(jnp.broadcast_to(inv, (D_HEAD, f)))
        q_scaled.append((query.astype(jnp.float32) * (inv_col * SCALE)).astype(jnp.bfloat16))
        g_scaled.append((grad.astype(jnp.float32) * inv_col).astype(jnp.bfloat16))
    q_both = jnp.concatenate(q_scaled, axis=0)
    g_both = jnp.concatenate(g_scaled, axis=0)
    delta_both = jnp.concatenate(delta_rows, axis=1)
    inv_both = jnp.concatenate(inv_rows, axis=1)
    dq_parts = [jnp.zeros((D_HEAD, f), jnp.float32) for _ in range(2)]
    outs = (
        (dl_ref, 0, tok), (dl_ref, f, tok + f),
        (dko_ref, 0, None), (dko_ref, f, None),
        (dr_ref, 0, tok), (dr_ref, f, tok + f),
        (dt_ref, 0, None),
    )
    for c, (k_ref, _, row, frames, _) in enumerate(chunks):
        rows = slice(c * f, (c + 1) * f)
        cols = slice(frames[0] * f, (frames[-1] + 1) * f)
        weights = e_scr[rows, cols]
        dscores = (weights.astype(jnp.float32) * (dp_scr[rows, cols] - delta_both[:, cols])).astype(jnp.bfloat16)
        value_term = dot(weights, g_both[cols], NN)
        key_term = dot(dscores, q_both[cols], NN)
        key = k_ref[row:row + f, :]
        for frame in frames:
            part = slice(frame * f - cols.start, (frame + 1) * f - cols.start)
            dq_parts[frame] = dq_parts[frame] + dot(key, dscores[:, part], TN)
        out_ref, at, value_at = outs[c]
        if out_ref is dko_ref:
            dko_ref[at:at + f, :] = key_term
            dvo_ref[at:at + f, :] = value_term
        elif out_ref is dt_ref:
            dt_ref[0, :, :] = key_term.astype(jnp.bfloat16)
            dt_ref[1, :, :] = value_term.astype(jnp.bfloat16)
        else:
            out_ref[at:at + f, :] = key_term.astype(jnp.bfloat16)
            out_ref[value_at:value_at + f, :] = value_term.astype(jnp.bfloat16)
    for frame in range(2):
        cols = slice(frame * f, (frame + 1) * f)
        query_grad = jnp.transpose(dq_parts[frame] * (inv_both[:, cols] * SCALE))
        dq_ref[cols, :] = unrotate(query_grad, cos_ref[cols, :], sin_ref[cols, :]).astype(jnp.bfloat16)


def attend(bias, cosine, sine, query, grad, key, value, left, right, text, before, first, heads):
    tok, width = query.shape
    txt = text.shape[0]
    all_heads = width // D_HEAD
    wide = heads * D_HEAD
    whole = lambda shape: pl.BlockSpec(shape, lambda h: (0, 0))
    here = pl.BlockSpec((tok, D_HEAD), lambda h: (0, first + h))
    upper = pl.BlockSpec((tok, D_HEAD), lambda h: (0, h))
    lower = pl.BlockSpec((tok, D_HEAD), lambda h: (1, h))
    text_k = pl.BlockSpec((txt, D_HEAD), lambda h: (0, first + h))
    text_v = pl.BlockSpec((txt, D_HEAD), lambda h: (0, all_heads + first + h))
    both = pl.BlockSpec((2 * tok, D_HEAD), lambda h: (0, h))
    in_specs = [whole(bias.shape), whole(cosine.shape), whole(sine.shape), here, here, here, here,
                upper, lower, upper, lower, text_k, text_v]
    operands = [bias, cosine, sine, query, grad, key, value, left, left, right, right, text, text]
    aliases = {}
    if before is not None:
        in_specs.append(pl.BlockSpec(memory_space=pl.ANY))
        operands.append(before)
        aliases = {len(operands) - 1: 0}
    keys = 3 * tok + txt
    pairs = tok * (5 * FRAME + txt) * heads
    return pl.pallas_call(
        functools.partial(attend_body, aliased=before is not None),
        grid=(heads,),
        in_specs=in_specs,
        out_specs=[here, upper, upper, both, both, pl.BlockSpec((2, txt, D_HEAD), lambda h: (0, 0, h))],
        out_shape=[
            jax.ShapeDtypeStruct((tok, width), jnp.bfloat16),
            jax.ShapeDtypeStruct((tok, wide), jnp.float32),
            jax.ShapeDtypeStruct((tok, wide), jnp.float32),
            jax.ShapeDtypeStruct((2 * tok, wide), jnp.bfloat16),
            jax.ShapeDtypeStruct((2 * tok, wide), jnp.bfloat16),
            jax.ShapeDtypeStruct((2, txt, wide), jnp.bfloat16),
        ],
        scratch_shapes=[
            pltpu.VMEM((keys, tok), jnp.float32),
            pltpu.VMEM((keys, tok), jnp.float32),
            pltpu.VMEM((keys, tok), jnp.bfloat16),
        ],
        input_output_aliases=aliases,
        compiler_params=pltpu.CompilerParams(vmem_limit_bytes=28 * 2**20),
        cost_estimate=pl.CostEstimate(flops=20 * pairs * D_HEAD, bytes_accessed=20 * tok * wide, transcendentals=pairs),
        name="attend",
    )(*operands)


def finish_body(*refs, aliased):
    cos_ref, sin_ref, dk_ref, dv_ref, lk_ref, lv_ref, rk_ref, rv_ref = refs[:8]
    key_ref, value_ref = refs[8 + (2 if aliased else 0):]
    up = lambda ref: ref[...].astype(jnp.float32)
    key_grad = dk_ref[...] + up(lk_ref) + up(rk_ref)
    key_ref[...] = unrotate(key_grad, cos_ref[...], sin_ref[...]).astype(jnp.bfloat16)
    value_ref[...] = (dv_ref[...] + up(lv_ref) + up(rv_ref)).astype(jnp.bfloat16)


def finish(cosine, sine, key_own, value_own, left_back, right_back, before, first, width):
    tok, wide = key_own.shape
    heads = wide // D_HEAD
    whole = pl.BlockSpec((tok, D_HEAD), lambda h: (0, 0))
    upper = pl.BlockSpec((tok, D_HEAD), lambda h: (0, h))
    lower = pl.BlockSpec((tok, D_HEAD), lambda h: (1, h))
    here = pl.BlockSpec((tok, D_HEAD), lambda h: (0, first + h))
    in_specs = [whole, whole, upper, upper, upper, lower, upper, lower]
    operands = [cosine, sine, key_own, value_own, left_back, left_back, right_back, right_back]
    aliases = {}
    if before is not None:
        in_specs += [pl.BlockSpec(memory_space=pl.ANY)] * 2
        operands += list(before)
        aliases = {8: 0, 9: 1}
    return pl.pallas_call(
        functools.partial(finish_body, aliased=before is not None),
        grid=(heads,),
        in_specs=in_specs,
        out_specs=[here, here],
        out_shape=[jax.ShapeDtypeStruct((tok, width), jnp.bfloat16)] * 2,
        input_output_aliases=aliases,
        compiler_params=pltpu.CompilerParams(vmem_limit_bytes=12 * 2**20),
        cost_estimate=pl.CostEstimate(flops=10 * tok * wide, bytes_accessed=20 * tok * wide, transcendentals=0),
        name="finish",
    )(*operands)


def shards(query_rot, key_rot, value, grad_out, text_key, text_value, positions, tile_mask):
    tok, width = query_rot.shape
    head_count = width // D_HEAD
    heads = head_count // GROUPS
    wide = heads * D_HEAD
    tiles = tok // TILE
    ctx_size = lax.axis_size("ctx")
    ctx_index = lax.axis_index("ctx")
    text_own = jnp.concatenate([text_key, text_value], axis=1)
    text = lax.all_to_all(jnp.tile(text_own, (ctx_size, 1)), "ctx", 0, 0, tiled=True)
    lefts, rights = [], []
    for group in range(GROUPS):
        cols = slice(group * wide, (group + 1) * wide)
        pair = jnp.concatenate([key_rot[:, cols], value[:, cols]], axis=0)
        lefts.append(shifted(pair, "ctx", 1))
        rights.append(shifted(pair, "ctx", -1))
    padded = jnp.pad(tile_mask, ((0, 0), (tiles, tiles)))
    block = lax.dynamic_slice(padded, (ctx_index * tiles, ctx_index * tiles), (tiles, 3 * tiles))
    bias = jnp.where(jnp.repeat(block.T > 0, TILE, axis=1), 0.0, BLOCKED).astype(jnp.float32)
    cosine, sine = rope_tables(positions)
    query_grad, outs, texts = None, [], []
    for group in range(GROUPS):
        query_grad, key_own, value_own, to_left, to_right, text_part = attend(
            bias, cosine, sine, query_rot, grad_out, key_rot, value, lefts[group], rights[group], text,
            query_grad, group * heads, heads)
        outs.append((key_own, value_own, shifted(to_right, "ctx", 1), shifted(to_left, "ctx", -1)))
        texts.append(lax.all_to_all(text_part, "ctx", 1, 1, tiled=True))
    done = None
    for group in range(GROUPS):
        done = finish(cosine, sine, *outs[group], done, group * heads, width)
    sums = [
        part.reshape(2, ctx_size, -1, wide).astype(jnp.float32).sum(axis=1).astype(jnp.bfloat16)
        for part in texts
    ]
    text_grads = jnp.concatenate(sums, axis=2)
    return query_grad, done[0], done[1], text_grads[0], text_grads[1]


def solution(mesh):
    spread = P("ctx", "tp")
    return jax.shard_map(
        shards,
        mesh=mesh,
        in_specs=(spread,) * 6 + (P(None, "ctx"), P()),
        out_specs=(spread,) * 5,
        check_vma=False,
    )
```

```python
import functools
import math

import jax
import jax.numpy as jnp
from jax import lax
from jax.experimental import pallas as pl
from jax.experimental.pallas import tpu as pltpu
from jax.sharding import PartitionSpec as P

D_HEAD = 128
TILE = 128
FRAME = 256
ROPE_THETA = 256.0
TIME_STRETCH = 0.25
SCALE = D_HEAD ** (-0.5)
EXP2_SCALE = SCALE * math.log2(math.e)
BLOCKED = 1e30
SPLIT = (1, 1)
NT = (((1,), (1,)), ((), ()))
NN = (((1,), (0,)), ((), ()))
TN = (((0,), (0,)), ((), ()))


def exchange(block, axis, first):
    size = lax.axis_size(axis)
    route = []
    for low in range(first, size - 1, 2):
        route += [(low, low + 1), (low + 1, low)]
    return lax.ppermute(block, axis, route)


def text_groups(size):
    run = min(8, size)
    near = [list(range(start, start + run)) for start in range(0, size, run)]
    far = [list(range(place, size, run)) for place in range(run)]
    return near, far


def swap(rows, groups):
    return lax.all_to_all(rows, "ctx", 0, 0, axis_index_groups=groups, tiled=True)


def part_sum(rows, parts):
    terms = rows.reshape(parts, -1, rows.shape[1]).astype(jnp.float32)
    return terms.sum(axis=0).astype(jnp.bfloat16)


def rope_tables(positions):
    time_dims = D_HEAD // 8
    plane_dims = (D_HEAD - time_dims) // 2
    layout = ((time_dims, TIME_STRETCH), (plane_dims, 1.0), (plane_dims, 1.0))
    angle_parts = []
    for axis_id in range(3):
        seg_width, stretch = layout[axis_id]
        pair_ids = (jnp.arange(seg_width, dtype=jnp.int32) // 2).astype(jnp.float32)
        frequency = ROPE_THETA ** (-2.0 * pair_ids / seg_width)
        scaled_pos = positions[axis_id].astype(jnp.float32) * stretch
        angle_parts.append(scaled_pos[:, None] * frequency[None, :])
    angles = jnp.concatenate(angle_parts, axis=1)
    odd = jnp.arange(D_HEAD, dtype=jnp.int32)[None, :] % 2 == 1
    sine = jnp.sin(angles)
    return jnp.cos(angles), jnp.where(odd, -sine, sine)


def unrotate(grad, cosine, sine):
    lane = lax.broadcasted_iota(jnp.int32, grad.shape, 1)
    partner = jnp.where(lane % 2 == 0, pltpu.roll(grad, D_HEAD - 1, 1), pltpu.roll(grad, 1, 1))
    return cosine * grad + sine * partner


def dot(lhs, rhs, dims):
    return lax.dot_general(lhs, rhs, dims, preferred_element_type=jnp.float32)


def fold_rows(block, combine):
    return combine(block.reshape(block.shape[0] // 8, 8, block.shape[1]), axis=0)


def by_place(rows):
    own, run = 8, 8
    tiles = rows.reshape(-1, run, own, rows.shape[1])
    return jnp.concatenate([tiles[r, place] for place in range(run) for r in range(tiles.shape[0])], axis=0)


def attend_body(*refs, aliased):
    (place_ref, bias_ref, cos_ref, sin_ref, q_ref, g_ref, ko_ref, vo_ref, ka_ref, va_ref, kb_ref, vb_ref, tk_ref,
     tv_ref) = refs[:14]
    refs = refs[14 + (1 if aliased else 0):]
    dq_ref, dko_ref, dvo_ref, da_ref, db_ref, dt_ref, s_scr, dp_scr, e_scr, kl_ref, vl_ref, kr_ref, vr_ref = refs
    even = place_ref[0] % 2 == 0
    for left_ref, right_ref, a_ref, b_ref in ((kl_ref, kr_ref, ka_ref, kb_ref), (vl_ref, vr_ref, va_ref, vb_ref)):
        left_ref[...] = jnp.where(even, b_ref[...], a_ref[...])
        right_ref[...] = jnp.where(even, a_ref[...], b_ref[...])
    tok = q_ref.shape[0]
    f = FRAME
    chunks = (
        (kl_ref, vl_ref, 0, (0,), 0),
        (kl_ref, vl_ref, f, (0, 1), 2),
        (ko_ref, vo_ref, 0, (0, 1), 4),
        (ko_ref, vo_ref, f, (0, 1), 6),
        (kr_ref, vr_ref, 0, (0, 1), 8),
        (kr_ref, vr_ref, f, (1,), 10),
        (tk_ref, tv_ref, 0, (0, 1), None),
    )
    inv_rows, delta_rows, q_scaled, g_scaled = [], [], [], []
    for frame in range(2):
        cols = slice(frame * f, (frame + 1) * f)
        query = q_ref[cols, :]
        grad = g_ref[cols, :]
        top = None
        for c, (k_ref, _, row, frames, tile) in enumerate(chunks):
            if frame not in frames:
                continue
            scores = dot(k_ref[row:row + f, :], query, NT)
            s_scr[c * f:(c + 1) * f, cols] = scores
            for t in range(2):
                part = fold_rows(scores[t * TILE:(t + 1) * TILE], jnp.max)
                if tile is not None:
                    part = part - bias_ref[tile + t:tile + t + 1, cols]
                top = part if top is None else jnp.maximum(top, part)
        top = jnp.max(top, axis=0, keepdims=True) * EXP2_SCALE
        total = jnp.zeros((8, f), jnp.float32)
        delta = jnp.zeros((8, f), jnp.float32)
        for c, (_, v_ref, row, frames, tile) in enumerate(chunks):
            if frame not in frames:
                continue
            dprobs = dot(v_ref[row:row + f, :], grad, NT)
            dp_scr[c * f:(c + 1) * f, cols] = dprobs
            for t in range(2):
                rows = slice(c * f + t * TILE, c * f + (t + 1) * TILE)
                shift = top
                if tile is not None:
                    shift = shift + bias_ref[tile + t:tile + t + 1, cols]
                weights = jnp.exp2(s_scr[rows, cols] * EXP2_SCALE - shift)
                e_scr[rows, cols] = weights.astype(jnp.bfloat16)
                total = total + fold_rows(weights, jnp.sum)
                delta = delta + fold_rows(weights * dprobs[t * TILE:(t + 1) * TILE], jnp.sum)
        inv = 1.0 / jnp.sum(total, axis=0, keepdims=True)
        delta_rows.append(jnp.sum(delta, axis=0, keepdims=True) * inv)
        inv_rows.append(inv)
        inv_col = jnp.transpose(jnp.broadcast_to(inv, (D_HEAD, f)))
        q_scaled.append((query.astype(jnp.float32) * (inv_col * SCALE)).astype(jnp.bfloat16))
        g_scaled.append((grad.astype(jnp.float32) * inv_col).astype(jnp.bfloat16))
    q_both = jnp.concatenate(q_scaled, axis=0)
    g_both = jnp.concatenate(g_scaled, axis=0)
    delta_both = jnp.concatenate(delta_rows, axis=1)
    inv_both = jnp.concatenate(inv_rows, axis=1)
    dq_parts = [jnp.zeros((D_HEAD, f), jnp.float32) for _ in range(2)]
    sides = {}
    for c, (k_ref, _, row, frames, _) in enumerate(chunks):
        rows = slice(c * f, (c + 1) * f)
        cols = slice(frames[0] * f, (frames[-1] + 1) * f)
        weights = e_scr[rows, cols]
        dscores = (weights.astype(jnp.float32) * (dp_scr[rows, cols] - delta_both[:, cols])).astype(jnp.bfloat16)
        value_term = dot(weights, g_both[cols], NN)
        key_term = dot(dscores, q_both[cols], NN)
        key = k_ref[row:row + f, :]
        for frame in frames:
            part = slice(frame * f - cols.start, (frame + 1) * f - cols.start)
            dq_parts[frame] = dq_parts[frame] + dot(key, dscores[:, part], TN)
        if k_ref is ko_ref:
            dko_ref[row:row + f, :] = key_term
            dvo_ref[row:row + f, :] = value_term
        elif k_ref is tk_ref:
            at = pl.multiple_of(pl.program_id(0) * D_HEAD, D_HEAD)
            value_at = pl.multiple_of(at + dt_ref.shape[1] // 2, D_HEAD)
            dt_ref[:, pl.ds(at, D_HEAD)] = by_place(key_term).astype(jnp.bfloat16)
            dt_ref[:, pl.ds(value_at, D_HEAD)] = by_place(value_term).astype(jnp.bfloat16)
        else:
            sides[k_ref is kr_ref, row] = key_term.astype(jnp.bfloat16), value_term.astype(jnp.bfloat16)
            if k_ref is kr_ref:
                for kind in range(2):
                    to_left, to_right = sides[False, row][kind], sides[True, row][kind]
                    rows = slice(kind * tok + row, kind * tok + row + f)
                    da_ref[rows, :] = jnp.where(even, to_right, to_left)
                    db_ref[rows, :] = jnp.where(even, to_left, to_right)
    for frame in range(2):
        cols = slice(frame * f, (frame + 1) * f)
        query_grad = jnp.transpose(dq_parts[frame] * (inv_both[:, cols] * SCALE))
        dq_ref[cols, :] = unrotate(query_grad, cos_ref[cols, :], sin_ref[cols, :]).astype(jnp.bfloat16)


def attend(place, bias, cosine, sine, query, grad, key, value, left, right, text, before, first, heads):
    tok, width = query.shape
    txt = text.shape[0]
    all_heads = width // D_HEAD
    wide = heads * D_HEAD
    whole = lambda shape: pl.BlockSpec(shape, lambda h: (0, 0))
    here = pl.BlockSpec((tok, D_HEAD), lambda h: (0, first + h))
    upper = pl.BlockSpec((tok, D_HEAD), lambda h: (0, h))
    lower = pl.BlockSpec((tok, D_HEAD), lambda h: (1, h))
    text_k = pl.BlockSpec((txt, D_HEAD), lambda h: (0, first + h))
    text_v = pl.BlockSpec((txt, D_HEAD), lambda h: (0, all_heads + first + h))
    both = pl.BlockSpec((2 * tok, D_HEAD), lambda h: (0, h))
    in_specs = [pl.BlockSpec(memory_space=pltpu.SMEM), whole(bias.shape), whole(cosine.shape), whole(sine.shape), here, here, here, here,
                upper, lower, upper, lower, text_k, text_v]
    operands = [place, bias, cosine, sine, query, grad, key, value, left, left, right, right, text, text]
    aliases = {}
    if before is not None:
        in_specs.append(pl.BlockSpec(memory_space=pl.ANY))
        operands.append(before)
        aliases = {len(operands) - 1: 0}
    keys = 3 * tok + txt
    pairs = tok * (5 * FRAME + txt) * heads
    return pl.pallas_call(
        functools.partial(attend_body, aliased=before is not None),
        grid=(heads,),
        in_specs=in_specs,
        out_specs=[here, upper, upper, both, both, whole((txt, 2 * wide))],
        out_shape=[
            jax.ShapeDtypeStruct((tok, width), jnp.bfloat16),
            jax.ShapeDtypeStruct((tok, wide), jnp.float32),
            jax.ShapeDtypeStruct((tok, wide), jnp.float32),
            jax.ShapeDtypeStruct((2 * tok, wide), jnp.bfloat16),
            jax.ShapeDtypeStruct((2 * tok, wide), jnp.bfloat16),
            jax.ShapeDtypeStruct((txt, 2 * wide), jnp.bfloat16),
        ],
        scratch_shapes=[
            pltpu.VMEM((keys, tok), jnp.float32),
            pltpu.VMEM((keys, tok), jnp.float32),
            pltpu.VMEM((keys, tok), jnp.bfloat16),
        ] + [pltpu.VMEM((tok, D_HEAD), jnp.bfloat16)] * 4,
        input_output_aliases=aliases,
        compiler_params=pltpu.CompilerParams(vmem_limit_bytes=56 * 2**20),
        cost_estimate=pl.CostEstimate(flops=pairs, bytes_accessed=tok * wide, transcendentals=0),
        name="attend",
    )(*operands)


def finish_body(*refs, aliased):
    cos_ref, sin_ref, dk_ref, dv_ref, ak_ref, av_ref, bk_ref, bv_ref = refs[:8]
    key_ref, value_ref = refs[8 + (2 if aliased else 0):]
    up = lambda ref, cols: ref[:, cols].astype(jnp.float32)
    cosine, sine = cos_ref[...], sin_ref[...]
    for head in range(dk_ref.shape[1] // D_HEAD):
        cols = slice(head * D_HEAD, (head + 1) * D_HEAD)
        key_grad = dk_ref[:, cols] + up(ak_ref, cols) + up(bk_ref, cols)
        key_ref[:, cols] = unrotate(key_grad, cosine, sine).astype(jnp.bfloat16)
        value_ref[:, cols] = (dv_ref[:, cols] + up(av_ref, cols) + up(bv_ref, cols)).astype(jnp.bfloat16)


def finish(cosine, sine, key_own, value_own, back_a, back_b, before, first, width):
    tok, wide = key_own.shape
    step = tok // 2
    upper = pl.BlockSpec((step, wide), lambda r: (r, 0))
    lower = pl.BlockSpec((step, wide), lambda r: (tok // step + r, 0))
    table = pl.BlockSpec((step, D_HEAD), lambda r: (r, 0))
    here = pl.BlockSpec((step, wide), lambda r: (r, first * D_HEAD // wide))
    in_specs = [table, table, upper, upper, upper, lower, upper, lower]
    operands = [cosine, sine, key_own, value_own, back_a, back_a, back_b, back_b]
    aliases = {}
    if before is not None:
        in_specs += [pl.BlockSpec(memory_space=pl.ANY)] * 2
        operands += list(before)
        aliases = {8: 0, 9: 1}
    return pl.pallas_call(
        functools.partial(finish_body, aliased=before is not None),
        grid=(tok // step,),
        in_specs=in_specs,
        out_specs=[here, here],
        out_shape=[jax.ShapeDtypeStruct((tok, width), jnp.bfloat16)] * 2,
        input_output_aliases=aliases,
        compiler_params=pltpu.CompilerParams(vmem_limit_bytes=56 * 2**20),
        cost_estimate=pl.CostEstimate(flops=10 * tok * wide, bytes_accessed=20 * tok * wide, transcendentals=0),
        name="finish",
    )(*operands)


def shards(query_rot, key_rot, value, grad_out, text_key, text_value, positions, tile_mask):
    tok, width = query_rot.shape
    head_count = width // D_HEAD
    sizes = [head_count * share // sum(SPLIT) for share in SPLIT]
    firsts = [sum(sizes[:group]) for group in range(len(sizes))]
    tiles = tok // TILE
    ctx_size = lax.axis_size("ctx")
    ctx_index = lax.axis_index("ctx")
    text_own = jnp.concatenate([text_key, text_value], axis=1)
    near, far = text_groups(ctx_size)

    def halo(keys, values, group):
        cols = slice(firsts[group] * D_HEAD, (firsts[group] + sizes[group]) * D_HEAD)
        pair = jnp.concatenate([keys[:, cols], values[:, cols]], axis=0)
        return exchange(pair, "ctx", 0), exchange(pair, "ctx", 1)

    halos = [halo(key_rot, value, 0)]
    text = lax.all_to_all(jnp.tile(text_own, (ctx_size, 1)), "ctx", 0, 0, tiled=True)
    text, keys_later, values_later = lax.optimization_barrier((text, key_rot, value))
    halos += [halo(keys_later, values_later, group) for group in range(1, len(sizes))]
    padded = jnp.pad(tile_mask, ((0, 0), (tiles, tiles)))
    block = lax.dynamic_slice(padded, (ctx_index * tiles, ctx_index * tiles), (tiles, 3 * tiles))
    bias = jnp.where(jnp.repeat(block.T > 0, TILE, axis=1), 0.0, BLOCKED).astype(jnp.float32)
    cosine, sine = rope_tables(positions)
    place = jnp.full((1,), ctx_index, jnp.int32)
    query_grad, waiting, done, near_texts = None, None, None, []
    for group, (first, heads) in enumerate(zip(firsts, sizes)):
        query_grad, key_own, value_own, to_even, to_odd, text_part = attend(
            place, bias, cosine, sine, query_rot, grad_out, key_rot, value, *halos[group], text,
            query_grad, first, heads)
        if waiting is not None:
            sent, ready = waiting[2:], (to_even, to_odd, text_part)
            sent, (to_even, to_odd, text_part) = lax.optimization_barrier((sent, ready))
            near_texts.append(sent[2])
            done = finish(cosine, sine, *waiting[:2], *sent[:2], done, firsts[group - 1], width)
        waiting = (key_own, value_own, exchange(to_even, "ctx", 0), exchange(to_odd, "ctx", 1), swap(text_part, near))
    near_texts.append(waiting[4])
    done = finish(cosine, sine, *waiting[:4], done, firsts[-1], width)
    near_sums = jnp.concatenate([part_sum(part, len(near[0])) for part in near_texts], axis=1)
    text_grads = part_sum(swap(near_sums, far), len(far[0]))
    starts = [2 * first * D_HEAD for first in firsts]
    text_key_grad, text_value_grad = (
        jnp.concatenate([text_grads[:, at + k * heads * D_HEAD:at + (k + 1) * heads * D_HEAD]
                         for at, heads in zip(starts, sizes)], axis=1)
        for k in range(2)
    )
    return query_grad, done[0], done[1], text_key_grad, text_value_grad


def solution(mesh):
    spread = P("ctx", "tp")
    return jax.shard_map(
        shards,
        mesh=mesh,
        in_specs=(spread,) * 6 + (P(None, "ctx"), P()),
        out_specs=(spread,) * 5,
        check_vma=False,
    )
```

```python
import functools
import math

import jax
import jax.numpy as jnp
from jax import lax
from jax.experimental import pallas as pl
from jax.experimental.pallas import tpu as pltpu
from jax.sharding import PartitionSpec as P

D_HEAD = 128
TILE = 128
FRAME = 256
ROPE_THETA = 256.0
TIME_STRETCH = 0.25
SCALE = D_HEAD ** (-0.5)
EXP2_SCALE = SCALE * math.log2(math.e)
BLOCKED = 1e30
SPLIT = (1, 1)
NT = (((1,), (1,)), ((), ()))
NN = (((1,), (0,)), ((), ()))
TN = (((0,), (0,)), ((), ()))


def exchange(block, axis, first):
    size = lax.axis_size(axis)
    route = []
    for low in range(first, size - 1, 2):
        route += [(low, low + 1), (low + 1, low)]
    return lax.ppermute(block, axis, route)


def text_groups(size):
    run = min(8, size)
    near = [list(range(start, start + run)) for start in range(0, size, run)]
    far = [list(range(place, size, run)) for place in range(run)]
    return near, far


def swap(rows, groups):
    return lax.all_to_all(rows, "ctx", 0, 0, axis_index_groups=groups, tiled=True)


def part_sum(rows, parts):
    terms = rows.reshape(parts, -1, rows.shape[1]).astype(jnp.float32)
    return terms.sum(axis=0).astype(jnp.bfloat16)


def rope_tables(positions):
    time_dims = D_HEAD // 8
    plane_dims = (D_HEAD - time_dims) // 2
    layout = ((time_dims, TIME_STRETCH), (plane_dims, 1.0), (plane_dims, 1.0))
    angle_parts = []
    for axis_id in range(3):
        seg_width, stretch = layout[axis_id]
        pair_ids = (jnp.arange(seg_width, dtype=jnp.int32) // 2).astype(jnp.float32)
        frequency = ROPE_THETA ** (-2.0 * pair_ids / seg_width)
        scaled_pos = positions[axis_id].astype(jnp.float32) * stretch
        angle_parts.append(scaled_pos[:, None] * frequency[None, :])
    angles = jnp.concatenate(angle_parts, axis=1)
    odd = jnp.arange(D_HEAD, dtype=jnp.int32)[None, :] % 2 == 1
    sine = jnp.sin(angles)
    return jnp.cos(angles), jnp.where(odd, -sine, sine)


def unrotate(grad, cosine, sine):
    lane = lax.broadcasted_iota(jnp.int32, grad.shape, 1)
    partner = jnp.where(lane % 2 == 0, pltpu.roll(grad, D_HEAD - 1, 1), pltpu.roll(grad, 1, 1))
    return cosine * grad + sine * partner


def dot(lhs, rhs, dims):
    return lax.dot_general(lhs, rhs, dims, preferred_element_type=jnp.float32)


def fold_rows(block, combine):
    return combine(block.reshape(block.shape[0] // 8, 8, block.shape[1]), axis=0)


def attend_body(*refs, aliased, txt_own):
    (place_ref, bias_ref, cos_ref, sin_ref, q_ref, g_ref, ko_ref, vo_ref, ka_ref, va_ref, kb_ref, vb_ref, tk_ref,
     tv_ref) = refs[:14]
    refs = refs[14 + (2 if aliased else 0):]
    dq_ref, do_ref, da_ref, db_ref, dt_ref, s_scr, dp_scr, e_scr, kl_ref, vl_ref, kr_ref, vr_ref = refs
    even = place_ref[0] % 2 == 0
    for left_ref, right_ref, a_ref, b_ref in ((kl_ref, kr_ref, ka_ref, kb_ref), (vl_ref, vr_ref, va_ref, vb_ref)):
        left_ref[...] = jnp.where(even, b_ref[...], a_ref[...])
        right_ref[...] = jnp.where(even, a_ref[...], b_ref[...])
    tok = q_ref.shape[0]
    f = FRAME
    chunks = (
        (kl_ref, vl_ref, 0, (0,), 0),
        (kl_ref, vl_ref, f, (0, 1), 2),
        (ko_ref, vo_ref, 0, (0, 1), 4),
        (ko_ref, vo_ref, f, (0, 1), 6),
        (kr_ref, vr_ref, 0, (0, 1), 8),
        (kr_ref, vr_ref, f, (1,), 10),
        (tk_ref, tv_ref, 0, (0, 1), None),
    )
    inv_rows, delta_rows, q_scaled, g_scaled = [], [], [], []
    for frame in range(2):
        cols = slice(frame * f, (frame + 1) * f)
        query = q_ref[cols, :]
        grad = g_ref[cols, :]
        top = None
        for c, (k_ref, _, row, frames, tile) in enumerate(chunks):
            if frame not in frames:
                continue
            scores = dot(k_ref[row:row + f, :], query, NT)
            s_scr[c * f:(c + 1) * f, cols] = scores
            for t in range(2):
                part = fold_rows(scores[t * TILE:(t + 1) * TILE], jnp.max)
                if tile is not None:
                    part = part - bias_ref[tile + t:tile + t + 1, cols]
                top = part if top is None else jnp.maximum(top, part)
        top = jnp.max(top, axis=0, keepdims=True) * EXP2_SCALE
        total = jnp.zeros((8, f), jnp.float32)
        delta = jnp.zeros((8, f), jnp.float32)
        for c, (_, v_ref, row, frames, tile) in enumerate(chunks):
            if frame not in frames:
                continue
            dprobs = dot(v_ref[row:row + f, :], grad, NT)
            dp_scr[c * f:(c + 1) * f, cols] = dprobs
            for t in range(2):
                rows = slice(c * f + t * TILE, c * f + (t + 1) * TILE)
                shift = top
                if tile is not None:
                    shift = shift + bias_ref[tile + t:tile + t + 1, cols]
                weights = jnp.exp2(s_scr[rows, cols] * EXP2_SCALE - shift)
                e_scr[rows, cols] = weights.astype(jnp.bfloat16)
                total = total + fold_rows(weights, jnp.sum)
                delta = delta + fold_rows(weights * dprobs[t * TILE:(t + 1) * TILE], jnp.sum)
        inv = 1.0 / jnp.sum(total, axis=0, keepdims=True)
        delta_rows.append(jnp.sum(delta, axis=0, keepdims=True) * inv)
        inv_rows.append(inv)
        inv_col = jnp.transpose(jnp.broadcast_to(inv, (D_HEAD, f)))
        q_scaled.append((query.astype(jnp.float32) * (inv_col * SCALE)).astype(jnp.bfloat16))
        g_scaled.append((grad.astype(jnp.float32) * inv_col).astype(jnp.bfloat16))
    q_both = jnp.concatenate(q_scaled, axis=0)
    g_both = jnp.concatenate(g_scaled, axis=0)
    delta_both = jnp.concatenate(delta_rows, axis=1)
    inv_both = jnp.concatenate(inv_rows, axis=1)
    dq_parts = [jnp.zeros((D_HEAD, f), jnp.float32) for _ in range(2)]
    sides = {}
    for c, (k_ref, _, row, frames, _) in enumerate(chunks):
        rows = slice(c * f, (c + 1) * f)
        cols = slice(frames[0] * f, (frames[-1] + 1) * f)
        weights = e_scr[rows, cols]
        dscores = (weights.astype(jnp.float32) * (dp_scr[rows, cols] - delta_both[:, cols])).astype(jnp.bfloat16)
        value_term = dot(weights, g_both[cols], NN)
        key_term = dot(dscores, q_both[cols], NN)
        key = k_ref[row:row + f, :]
        for frame in frames:
            part = slice(frame * f - cols.start, (frame + 1) * f - cols.start)
            dq_parts[frame] = dq_parts[frame] + dot(key, dscores[:, part], TN)
        if k_ref is ko_ref:
            do_ref[row:row + f, :] = key_term.astype(jnp.bfloat16)
            do_ref[tok + row:tok + row + f, :] = value_term.astype(jnp.bfloat16)
        elif k_ref is tk_ref:
            own = txt_own
            pair = jnp.stack([term.reshape(-1, own, D_HEAD) for term in (key_term, value_term)], axis=1)
            dt_ref[...] = pair.reshape(dt_ref.shape).astype(jnp.bfloat16)
        else:
            sides[k_ref is kr_ref, row] = key_term.astype(jnp.bfloat16), value_term.astype(jnp.bfloat16)
            if k_ref is kr_ref:
                for kind in range(2):
                    to_left, to_right = sides[False, row][kind], sides[True, row][kind]
                    rows = slice(kind * tok + row, kind * tok + row + f)
                    da_ref[rows, :] = jnp.where(even, to_right, to_left)
                    db_ref[rows, :] = jnp.where(even, to_left, to_right)
    for frame in range(2):
        cols = slice(frame * f, (frame + 1) * f)
        query_grad = jnp.transpose(dq_parts[frame] * (inv_both[:, cols] * SCALE))
        dq_ref[cols, :] = unrotate(query_grad, cos_ref[cols, :], sin_ref[cols, :]).astype(jnp.bfloat16)


def attend(txt_own, place, bias, cosine, sine, query, grad, key, value, left, right, text, before, first, heads):
    tok, width = query.shape
    txt = text.shape[0]
    all_heads = width // D_HEAD
    wide = heads * D_HEAD
    whole = lambda shape: pl.BlockSpec(shape, lambda h: (0, 0))
    here = pl.BlockSpec((tok, D_HEAD), lambda h: (0, first + h))
    upper = pl.BlockSpec((tok, D_HEAD), lambda h: (0, h))
    lower = pl.BlockSpec((tok, D_HEAD), lambda h: (1, h))
    text_k = pl.BlockSpec((txt, D_HEAD), lambda h: (0, first + h))
    text_v = pl.BlockSpec((txt, D_HEAD), lambda h: (0, all_heads + first + h))
    both = pl.BlockSpec((2 * tok, D_HEAD), lambda h: (0, h))
    in_specs = [pl.BlockSpec(memory_space=pltpu.SMEM), whole(bias.shape), whole(cosine.shape), whole(sine.shape), here, here, here, here,
                upper, lower, upper, lower, text_k, text_v]
    operands = [place, bias, cosine, sine, query, grad, key, value, left, left, right, right, text, text]
    aliases = {}
    if before is not None:
        aliases = {len(operands): 0, len(operands) + 1: 4}
        in_specs += [pl.BlockSpec(memory_space=pl.ANY)] * 2
        operands += list(before)
    keys = 3 * tok + txt
    pairs = tok * (5 * FRAME + txt) * heads
    return pl.pallas_call(
        functools.partial(attend_body, aliased=before is not None, txt_own=txt_own),
        grid=(heads,),
        in_specs=in_specs,
        out_specs=[here, both, both, both, pl.BlockSpec((2 * txt, D_HEAD), lambda h: (0, first + h))],
        out_shape=[
            jax.ShapeDtypeStruct((tok, width), jnp.bfloat16),
            jax.ShapeDtypeStruct((2 * tok, wide), jnp.bfloat16),
            jax.ShapeDtypeStruct((2 * tok, wide), jnp.bfloat16),
            jax.ShapeDtypeStruct((2 * tok, wide), jnp.bfloat16),
            jax.ShapeDtypeStruct((2 * txt, width), jnp.bfloat16),
        ],
        scratch_shapes=[
            pltpu.VMEM((keys, tok), jnp.float32),
            pltpu.VMEM((keys, tok), jnp.float32),
            pltpu.VMEM((keys, tok), jnp.bfloat16),
        ] + [pltpu.VMEM((tok, D_HEAD), jnp.bfloat16)] * 4,
        input_output_aliases=aliases,
        compiler_params=pltpu.CompilerParams(vmem_limit_bytes=56 * 2**20),
        cost_estimate=pl.CostEstimate(flops=pairs, bytes_accessed=tok * wide, transcendentals=0),
        name="attend",
    )(*operands)


def finish_body(*refs, aliased):
    cos_ref, sin_ref, ok_ref, ov_ref, ak_ref, av_ref, bk_ref, bv_ref = refs[:8]
    key_ref, value_ref = refs[8 + (2 if aliased else 0):]
    up = lambda ref, cols: ref[:, cols].astype(jnp.float32)
    cosine, sine = cos_ref[...], sin_ref[...]
    for head in range(ok_ref.shape[1] // D_HEAD):
        cols = slice(head * D_HEAD, (head + 1) * D_HEAD)
        key_grad = up(ok_ref, cols) + up(ak_ref, cols) + up(bk_ref, cols)
        key_ref[:, cols] = unrotate(key_grad, cosine, sine).astype(jnp.bfloat16)
        value_ref[:, cols] = (up(ov_ref, cols) + up(av_ref, cols) + up(bv_ref, cols)).astype(jnp.bfloat16)


def finish(cosine, sine, own, back_a, back_b, before, first, width):
    tok, wide = own.shape[0] // 2, own.shape[1]
    step = tok // 2
    upper = pl.BlockSpec((step, wide), lambda r: (r, 0))
    lower = pl.BlockSpec((step, wide), lambda r: (tok // step + r, 0))
    table = pl.BlockSpec((step, D_HEAD), lambda r: (r, 0))
    here = pl.BlockSpec((step, wide), lambda r: (r, first * D_HEAD // wide))
    in_specs = [table, table] + [upper, lower] * 3
    operands = [cosine, sine, own, own, back_a, back_a, back_b, back_b]
    aliases = {}
    if before is not None:
        in_specs += [pl.BlockSpec(memory_space=pl.ANY)] * 2
        operands += list(before)
        aliases = {8: 0, 9: 1}
    return pl.pallas_call(
        functools.partial(finish_body, aliased=before is not None),
        grid=(tok // step,),
        in_specs=in_specs,
        out_specs=[here, here],
        out_shape=[jax.ShapeDtypeStruct((tok, width), jnp.bfloat16)] * 2,
        input_output_aliases=aliases,
        compiler_params=pltpu.CompilerParams(vmem_limit_bytes=16 * 2**20),
        cost_estimate=pl.CostEstimate(flops=10 * tok * wide, bytes_accessed=20 * tok * wide, transcendentals=0),
        name="finish",
    )(*operands)


def shards(query_rot, key_rot, value, grad_out, text_key, text_value, positions, tile_mask):
    tok, width = query_rot.shape
    head_count = width // D_HEAD
    sizes = [head_count * share // sum(SPLIT) for share in SPLIT]
    firsts = [sum(sizes[:group]) for group in range(len(sizes))]
    tiles = tok // TILE
    ctx_size = lax.axis_size("ctx")
    ctx_index = lax.axis_index("ctx")
    text_own = jnp.concatenate([text_key, text_value], axis=1)
    near, far = text_groups(ctx_size)

    def halo(keys, values, group):
        cols = slice(firsts[group] * D_HEAD, (firsts[group] + sizes[group]) * D_HEAD)
        pair = jnp.concatenate([keys[:, cols], values[:, cols]], axis=0)
        return exchange(pair, "ctx", 0), exchange(pair, "ctx", 1)

    halos = [halo(key_rot, value, 0)]
    text = lax.all_to_all(jnp.tile(text_own, (ctx_size, 1)), "ctx", 0, 0, tiled=True)
    padded = jnp.pad(tile_mask, ((0, 0), (tiles, tiles)))
    block = lax.dynamic_slice(padded, (ctx_index * tiles, ctx_index * tiles), (tiles, 3 * tiles))
    bias = jnp.where(jnp.repeat(block.T > 0, TILE, axis=1), 0.0, BLOCKED).astype(jnp.float32)
    tables = rope_tables(positions)
    halos[0], (cosine, sine), bias, keys_later, values_later = lax.optimization_barrier(
        (halos[0], tables, bias, key_rot, value))
    halos += [halo(keys_later, values_later, group) for group in range(1, len(sizes))]
    place = jnp.full((1,), ctx_index, jnp.int32)
    before, waiting, done = None, None, None
    for group, (first, heads) in enumerate(zip(firsts, sizes)):
        query_grad, own, to_even, to_odd, text_part = attend(
            text_key.shape[0], place, bias, cosine, sine, query_rot, grad_out, key_rot, value, *halos[group], text,
            before, first, heads)
        if waiting is not None:
            done = finish(cosine, sine, *waiting, done, firsts[group - 1], width)
        before = query_grad, text_part
        waiting = (own, exchange(to_even, "ctx", 0), exchange(to_odd, "ctx", 1))
    done = finish(cosine, sine, *waiting, done, firsts[-1], width)

    def reduce_text(rows):
        return part_sum(lax.all_to_all(rows, "ctx", 0, 0, tiled=True), ctx_size)

    own = text_key.shape[0]
    passes = jnp.minimum(tile_mask[0, 0] + 1, 1)
    text_grads = lax.fori_loop(
        0, passes, lambda step, _: reduce_text(lax.optimization_barrier((text_part, step))[0]), text_part[:2 * own])
    return query_grad, done[0], done[1], text_grads[:own], text_grads[own:]


def solution(mesh):
    spread = P("ctx", "tp")
    return jax.shard_map(
        shards,
        mesh=mesh,
        in_specs=(spread,) * 6 + (P(None, "ctx"), P()),
        out_specs=(spread,) * 5,
        check_vma=False,
    )
```

```python
import functools
import math

import jax
import jax.numpy as jnp
from jax import lax
from jax.experimental import pallas as pl
from jax.experimental.pallas import tpu as pltpu
from jax.sharding import PartitionSpec as P

D_HEAD = 128
TILE = 128
FRAME = 256
ROPE_THETA = 256.0
TIME_STRETCH = 0.25
SCALE = D_HEAD ** (-0.5)
EXP2_SCALE = SCALE * math.log2(math.e)
BLOCKED = 1e30
SPLIT = (1, 1)
NT = (((1,), (1,)), ((), ()))
NN = (((1,), (0,)), ((), ()))
TN = (((0,), (0,)), ((), ()))


def exchange(block, axis, first):
    size = lax.axis_size(axis)
    route = []
    for low in range(first, size - 1, 2):
        route += [(low, low + 1), (low + 1, low)]
    return lax.ppermute(block, axis, route)


def text_groups(size):
    run = min(8, size)
    near = [list(range(start, start + run)) for start in range(0, size, run)]
    far = [list(range(place, size, run)) for place in range(run)]
    return near, far


def swap(rows, groups):
    return lax.all_to_all(rows, "ctx", 0, 0, axis_index_groups=groups, tiled=True)


def part_sum(rows, parts):
    terms = rows.reshape(parts, -1, rows.shape[1]).astype(jnp.float32)
    return terms.sum(axis=0).astype(jnp.bfloat16)


def rope_tables(positions):
    time_dims = D_HEAD // 8
    plane_dims = (D_HEAD - time_dims) // 2
    layout = ((time_dims, TIME_STRETCH), (plane_dims, 1.0), (plane_dims, 1.0))
    angle_parts = []
    for axis_id in range(3):
        seg_width, stretch = layout[axis_id]
        pair_ids = (jnp.arange(seg_width, dtype=jnp.int32) // 2).astype(jnp.float32)
        frequency = ROPE_THETA ** (-2.0 * pair_ids / seg_width)
        scaled_pos = positions[axis_id].astype(jnp.float32) * stretch
        angle_parts.append(scaled_pos[:, None] * frequency[None, :])
    angles = jnp.concatenate(angle_parts, axis=1)
    odd = jnp.arange(D_HEAD, dtype=jnp.int32)[None, :] % 2 == 1
    sine = jnp.sin(angles)
    return jnp.cos(angles), jnp.where(odd, -sine, sine)


def unrotate(grad, cosine, sine):
    lane = lax.broadcasted_iota(jnp.int32, grad.shape, 1)
    partner = jnp.where(lane % 2 == 0, pltpu.roll(grad, D_HEAD - 1, 1), pltpu.roll(grad, 1, 1))
    return cosine * grad + sine * partner


def dot(lhs, rhs, dims):
    return lax.dot_general(lhs, rhs, dims, preferred_element_type=jnp.float32)


def fold_rows(block, combine):
    return combine(block.reshape(block.shape[0] // 8, 8, block.shape[1]), axis=0)


def attend_body(*refs, aliased, txt_own):
    (place_ref, bias_ref, cos_ref, sin_ref, q_ref, g_ref, ko_ref, vo_ref, ka_ref, va_ref, kb_ref, vb_ref, tk_ref,
     tv_ref) = refs[:14]
    refs = refs[14 + (2 if aliased else 0):]
    dq_ref, do_ref, da_ref, db_ref, dt_ref, s_scr, dp_scr, e_scr, kl_ref, vl_ref, kr_ref, vr_ref = refs
    even = place_ref[0] % 2 == 0
    for left_ref, right_ref, a_ref, b_ref in ((kl_ref, kr_ref, ka_ref, kb_ref), (vl_ref, vr_ref, va_ref, vb_ref)):
        left_ref[...] = jnp.where(even, b_ref[...], a_ref[...])
        right_ref[...] = jnp.where(even, a_ref[...], b_ref[...])
    tok = q_ref.shape[0]
    f = FRAME
    chunks = (
        (kl_ref, vl_ref, 0, (0,), 0),
        (kl_ref, vl_ref, f, (0, 1), 2),
        (ko_ref, vo_ref, 0, (0, 1), 4),
        (ko_ref, vo_ref, f, (0, 1), 6),
        (kr_ref, vr_ref, 0, (0, 1), 8),
        (kr_ref, vr_ref, f, (1,), 10),
        (tk_ref, tv_ref, 0, (0, 1), None),
    )
    inv_rows, delta_rows, q_scaled, g_scaled = [], [], [], []
    for frame in range(2):
        cols = slice(frame * f, (frame + 1) * f)
        query = q_ref[cols, :]
        grad = g_ref[cols, :]
        top = None
        for c, (k_ref, _, row, frames, tile) in enumerate(chunks):
            if frame not in frames:
                continue
            scores = dot(k_ref[row:row + f, :], query, NT)
            s_scr[c * f:(c + 1) * f, cols] = scores
            for t in range(2):
                part = fold_rows(scores[t * TILE:(t + 1) * TILE], jnp.max)
                if tile is not None:
                    part = part - bias_ref[tile + t:tile + t + 1, cols]
                top = part if top is None else jnp.maximum(top, part)
        top = jnp.max(top, axis=0, keepdims=True) * EXP2_SCALE
        total = jnp.zeros((8, f), jnp.float32)
        delta = jnp.zeros((8, f), jnp.float32)
        for c, (_, v_ref, row, frames, tile) in enumerate(chunks):
            if frame not in frames:
                continue
            dprobs = dot(v_ref[row:row + f, :], grad, NT)
            dp_scr[c * f:(c + 1) * f, cols] = dprobs
            for t in range(2):
                rows = slice(c * f + t * TILE, c * f + (t + 1) * TILE)
                shift = top
                if tile is not None:
                    shift = shift + bias_ref[tile + t:tile + t + 1, cols]
                weights = jnp.exp2(s_scr[rows, cols] * EXP2_SCALE - shift)
                e_scr[rows, cols] = weights.astype(jnp.bfloat16)
                total = total + fold_rows(weights, jnp.sum)
                delta = delta + fold_rows(weights * dprobs[t * TILE:(t + 1) * TILE], jnp.sum)
        inv = 1.0 / jnp.sum(total, axis=0, keepdims=True)
        delta_rows.append(jnp.sum(delta, axis=0, keepdims=True) * inv)
        inv_rows.append(inv)
        inv_col = jnp.transpose(jnp.broadcast_to(inv, (D_HEAD, f)))
        q_scaled.append((query.astype(jnp.float32) * (inv_col * SCALE)).astype(jnp.bfloat16))
        g_scaled.append((grad.astype(jnp.float32) * inv_col).astype(jnp.bfloat16))
    q_both = jnp.concatenate(q_scaled, axis=0)
    g_both = jnp.concatenate(g_scaled, axis=0)
    delta_both = jnp.concatenate(delta_rows, axis=1)
    inv_both = jnp.concatenate(inv_rows, axis=1)
    dq_parts = [jnp.zeros((D_HEAD, f), jnp.float32) for _ in range(2)]
    sides = {}
    for c, (k_ref, _, row, frames, _) in enumerate(chunks):
        rows = slice(c * f, (c + 1) * f)
        cols = slice(frames[0] * f, (frames[-1] + 1) * f)
        weights = e_scr[rows, cols]
        dscores = (weights.astype(jnp.float32) * (dp_scr[rows, cols] - delta_both[:, cols])).astype(jnp.bfloat16)
        value_term = dot(weights, g_both[cols], NN)
        key_term = dot(dscores, q_both[cols], NN)
        key = k_ref[row:row + f, :]
        for frame in frames:
            part = slice(frame * f - cols.start, (frame + 1) * f - cols.start)
            dq_parts[frame] = dq_parts[frame] + dot(key, dscores[:, part], TN)
        if k_ref is ko_ref:
            do_ref[row:row + f, :] = key_term.astype(jnp.bfloat16)
            do_ref[tok + row:tok + row + f, :] = value_term.astype(jnp.bfloat16)
        elif k_ref is tk_ref:
            own = txt_own
            pair = jnp.stack([term.reshape(-1, own, D_HEAD) for term in (key_term, value_term)], axis=1)
            dt_ref[...] = pair.reshape(dt_ref.shape).astype(jnp.bfloat16)
        else:
            sides[k_ref is kr_ref, row] = key_term.astype(jnp.bfloat16), value_term.astype(jnp.bfloat16)
            if k_ref is kr_ref:
                for kind in range(2):
                    to_left, to_right = sides[False, row][kind], sides[True, row][kind]
                    rows = slice(kind * tok + row, kind * tok + row + f)
                    da_ref[rows, :] = jnp.where(even, to_right, to_left)
                    db_ref[rows, :] = jnp.where(even, to_left, to_right)
    for frame in range(2):
        cols = slice(frame * f, (frame + 1) * f)
        query_grad = jnp.transpose(dq_parts[frame] * (inv_both[:, cols] * SCALE))
        dq_ref[cols, :] = unrotate(query_grad, cos_ref[cols, :], sin_ref[cols, :]).astype(jnp.bfloat16)


def attend(txt_own, place, bias, cosine, sine, query, grad, key, value, left, right, text, before, first, heads):
    tok, width = query.shape
    txt = text.shape[0]
    all_heads = width // D_HEAD
    wide = heads * D_HEAD
    whole = lambda shape: pl.BlockSpec(shape, lambda h: (0, 0))
    here = pl.BlockSpec((tok, D_HEAD), lambda h: (0, first + h))
    upper = pl.BlockSpec((tok, D_HEAD), lambda h: (0, h))
    lower = pl.BlockSpec((tok, D_HEAD), lambda h: (1, h))
    text_k = pl.BlockSpec((txt, D_HEAD), lambda h: (0, first + h))
    text_v = pl.BlockSpec((txt, D_HEAD), lambda h: (0, all_heads + first + h))
    both = pl.BlockSpec((2 * tok, D_HEAD), lambda h: (0, h))
    in_specs = [pl.BlockSpec(memory_space=pltpu.SMEM), whole(bias.shape), whole(cosine.shape), whole(sine.shape), here, here, here, here,
                upper, lower, upper, lower, text_k, text_v]
    operands = [place, bias, cosine, sine, query, grad, key, value, left, left, right, right, text, text]
    aliases = {}
    if before is not None:
        aliases = {len(operands): 0, len(operands) + 1: 4}
        in_specs += [pl.BlockSpec(memory_space=pl.ANY)] * 2
        operands += list(before)
    keys = 3 * tok + txt
    pairs = tok * (5 * FRAME + txt) * heads
    return pl.pallas_call(
        functools.partial(attend_body, aliased=before is not None, txt_own=txt_own),
        grid=(heads,),
        in_specs=in_specs,
        out_specs=[here, both, both, both, pl.BlockSpec((2 * txt, D_HEAD), lambda h: (0, first + h))],
        out_shape=[
            jax.ShapeDtypeStruct((tok, width), jnp.bfloat16),
            jax.ShapeDtypeStruct((2 * tok, wide), jnp.bfloat16),
            jax.ShapeDtypeStruct((2 * tok, wide), jnp.bfloat16),
            jax.ShapeDtypeStruct((2 * tok, wide), jnp.bfloat16),
            jax.ShapeDtypeStruct((2 * txt, width), jnp.bfloat16),
        ],
        scratch_shapes=[
            pltpu.VMEM((keys, tok), jnp.float32),
            pltpu.VMEM((keys, tok), jnp.float32),
            pltpu.VMEM((keys, tok), jnp.bfloat16),
        ] + [pltpu.VMEM((tok, D_HEAD), jnp.bfloat16)] * 4,
        input_output_aliases=aliases,
        compiler_params=pltpu.CompilerParams(vmem_limit_bytes=60 * 2**20),
        cost_estimate=pl.CostEstimate(flops=pairs, bytes_accessed=tok * wide, transcendentals=0),
        name="attend",
    )(*operands)


def finish_body(*refs, aliased):
    cos_ref, sin_ref, ok_ref, ov_ref, ak_ref, av_ref, bk_ref, bv_ref = refs[:8]
    key_ref, value_ref = refs[8 + (2 if aliased else 0):]
    up = lambda ref, cols: ref[:, cols].astype(jnp.float32)
    cosine, sine = cos_ref[...], sin_ref[...]
    for head in range(ok_ref.shape[1] // D_HEAD):
        cols = slice(head * D_HEAD, (head + 1) * D_HEAD)
        key_grad = up(ok_ref, cols) + up(ak_ref, cols) + up(bk_ref, cols)
        key_ref[:, cols] = unrotate(key_grad, cosine, sine).astype(jnp.bfloat16)
        value_ref[:, cols] = (up(ov_ref, cols) + up(av_ref, cols) + up(bv_ref, cols)).astype(jnp.bfloat16)


def finish(cosine, sine, own, back_a, back_b, before, first, width):
    tok, wide = own.shape[0] // 2, own.shape[1]
    step = tok // 2
    upper = pl.BlockSpec((step, wide), lambda r: (r, 0))
    lower = pl.BlockSpec((step, wide), lambda r: (tok // step + r, 0))
    table = pl.BlockSpec((step, D_HEAD), lambda r: (r, 0))
    here = pl.BlockSpec((step, wide), lambda r: (r, first * D_HEAD // wide))
    in_specs = [table, table] + [upper, lower] * 3
    operands = [cosine, sine, own, own, back_a, back_a, back_b, back_b]
    aliases = {}
    if before is not None:
        in_specs += [pl.BlockSpec(memory_space=pl.ANY)] * 2
        operands += list(before)
        aliases = {8: 0, 9: 1}
    return pl.pallas_call(
        functools.partial(finish_body, aliased=before is not None),
        grid=(tok // step,),
        in_specs=in_specs,
        out_specs=[here, here],
        out_shape=[jax.ShapeDtypeStruct((tok, width), jnp.bfloat16)] * 2,
        input_output_aliases=aliases,
        compiler_params=pltpu.CompilerParams(vmem_limit_bytes=16 * 2**20),
        cost_estimate=pl.CostEstimate(flops=10 * tok * wide, bytes_accessed=20 * tok * wide, transcendentals=0),
        name="finish",
    )(*operands)


def shards(query_rot, key_rot, value, grad_out, text_key, text_value, positions, tile_mask):
    tok, width = query_rot.shape
    head_count = width // D_HEAD
    sizes = [head_count * share // sum(SPLIT) for share in SPLIT]
    firsts = [sum(sizes[:group]) for group in range(len(sizes))]
    tiles = tok // TILE
    ctx_size = lax.axis_size("ctx")
    ctx_index = lax.axis_index("ctx")
    text_own = jnp.concatenate([text_key, text_value], axis=1)
    near, far = text_groups(ctx_size)

    def packed(keys, values, group):
        cols = slice(firsts[group] * D_HEAD, (firsts[group] + sizes[group]) * D_HEAD)
        return jnp.concatenate([keys[:, cols], values[:, cols]], axis=0)

    pair = packed(key_rot, value, 0)
    halos = [(exchange(pair, "ctx", 0), exchange(pair, "ctx", 1))]
    text = lax.all_to_all(jnp.tile(text_own, (ctx_size, 1)), "ctx", 0, 0, tiled=True)
    padded = jnp.pad(tile_mask, ((0, 0), (tiles, tiles)))
    block = lax.dynamic_slice(padded, (ctx_index * tiles, ctx_index * tiles), (tiles, 3 * tiles))
    bias = jnp.where(jnp.repeat(block.T > 0, TILE, axis=1), 0.0, BLOCKED).astype(jnp.float32)
    tables = rope_tables(positions)
    near_pair, keys_later, values_later = lax.optimization_barrier((halos[0][0], key_rot, value))
    pairs = [packed(keys_later, values_later, group) for group in range(1, len(sizes))]
    first_halves = [exchange(pair, "ctx", 0) for pair in pairs]
    far_pair, (cosine, sine), bias, pairs = lax.optimization_barrier((halos[0][1], tables, bias, pairs))
    halos = [(near_pair, far_pair)] + [(half, exchange(pair, "ctx", 1)) for half, pair in zip(first_halves, pairs)]
    place = jnp.full((1,), ctx_index, jnp.int32)
    before, waiting, done = None, None, None
    for group, (first, heads) in enumerate(zip(firsts, sizes)):
        query_grad, own, to_even, to_odd, text_part = attend(
            text_key.shape[0], place, bias, cosine, sine, query_rot, grad_out, key_rot, value, *halos[group], text,
            before, first, heads)
        if waiting is not None:
            done = finish(cosine, sine, *waiting, done, firsts[group - 1], width)
        before = query_grad, text_part
        waiting = (own, exchange(to_even, "ctx", 0), exchange(to_odd, "ctx", 1))
    done = finish(cosine, sine, *waiting, done, firsts[-1], width)

    def reduce_text(rows):
        return part_sum(lax.all_to_all(rows, "ctx", 0, 0, tiled=True), ctx_size)

    own = text_key.shape[0]
    passes = jnp.minimum(tile_mask[0, 0] + 1, 1)
    text_grads = lax.fori_loop(
        0, passes, lambda step, _: reduce_text(lax.optimization_barrier((text_part, step))[0]), jnp.concatenate([text_key, text_value], axis=0))
    return query_grad, done[0], done[1], text_grads[:own], text_grads[own:]


def solution(mesh):
    spread = P("ctx", "tp")
    return jax.shard_map(
        shards,
        mesh=mesh,
        in_specs=(spread,) * 6 + (P(None, "ctx"), P()),
        out_specs=(spread,) * 5,
        check_vma=False,
    )
```

```python
import functools
import math

import jax
import jax.numpy as jnp
from jax import lax
from jax.experimental import pallas as pl
from jax.experimental.pallas import tpu as pltpu
from jax.sharding import PartitionSpec as P

D_HEAD = 128
TILE = 128
FRAME = 256
ROPE_THETA = 256.0
TIME_STRETCH = 0.25
SCALE = D_HEAD ** (-0.5)
EXP2_SCALE = SCALE * math.log2(math.e)
BLOCKED = 1e30
SPLIT = (1, 1)
NT = (((1,), (1,)), ((), ()))
NN = (((1,), (0,)), ((), ()))
TN = (((0,), (0,)), ((), ()))


def exchange(block, axis, first):
    size = lax.axis_size(axis)
    route = []
    for low in range(first, size - 1, 2):
        route += [(low, low + 1), (low + 1, low)]
    return lax.ppermute(block, axis, route)


def text_groups(size):
    run = min(8, size)
    near = [list(range(start, start + run)) for start in range(0, size, run)]
    far = [list(range(place, size, run)) for place in range(run)]
    return near, far


def swap(rows, groups):
    return lax.all_to_all(rows, "ctx", 0, 0, axis_index_groups=groups, tiled=True)


def part_sum(rows, parts):
    terms = rows.reshape(parts, -1, rows.shape[1]).astype(jnp.float32)
    return terms.sum(axis=0).astype(jnp.bfloat16)


def rope_tables(positions):
    time_dims = D_HEAD // 8
    plane_dims = (D_HEAD - time_dims) // 2
    layout = ((time_dims, TIME_STRETCH), (plane_dims, 1.0), (plane_dims, 1.0))
    angle_parts = []
    for axis_id in range(3):
        seg_width, stretch = layout[axis_id]
        pair_ids = (jnp.arange(seg_width, dtype=jnp.int32) // 2).astype(jnp.float32)
        frequency = ROPE_THETA ** (-2.0 * pair_ids / seg_width)
        scaled_pos = positions[axis_id].astype(jnp.float32) * stretch
        angle_parts.append(scaled_pos[:, None] * frequency[None, :])
    angles = jnp.concatenate(angle_parts, axis=1)
    odd = jnp.arange(D_HEAD, dtype=jnp.int32)[None, :] % 2 == 1
    sine = jnp.sin(angles)
    return jnp.cos(angles), jnp.where(odd, -sine, sine)


def unrotate(grad, cosine, sine):
    lane = lax.broadcasted_iota(jnp.int32, grad.shape, 1)
    partner = jnp.where(lane % 2 == 0, pltpu.roll(grad, D_HEAD - 1, 1), pltpu.roll(grad, 1, 1))
    return cosine * grad + sine * partner


def dot(lhs, rhs, dims):
    return lax.dot_general(lhs, rhs, dims, preferred_element_type=jnp.float32)


def fold_rows(block, combine):
    return combine(block.reshape(block.shape[0] // 8, 8, block.shape[1]), axis=0)


def attend_body(*refs, aliased, txt_own):
    (place_ref, bias_ref, cos_ref, sin_ref, q_ref, g_ref, ko_ref, vo_ref, ka_ref, va_ref, kb_ref, vb_ref, tk_ref,
     tv_ref) = refs[:14]
    refs = refs[14 + (2 if aliased else 0):]
    dq_ref, do_ref, da_ref, db_ref, dt_ref, s_scr, dp_scr, e_scr, kl_ref, vl_ref, kr_ref, vr_ref = refs
    even = place_ref[0] % 2 == 0
    for left_ref, right_ref, a_ref, b_ref in ((kl_ref, kr_ref, ka_ref, kb_ref), (vl_ref, vr_ref, va_ref, vb_ref)):
        left_ref[...] = jnp.where(even, b_ref[...], a_ref[...])
        right_ref[...] = jnp.where(even, a_ref[...], b_ref[...])
    tok = q_ref.shape[0]
    f = FRAME
    chunks = (
        (kl_ref, vl_ref, 0, (0,), 0),
        (kl_ref, vl_ref, f, (0, 1), 2),
        (ko_ref, vo_ref, 0, (0, 1), 4),
        (ko_ref, vo_ref, f, (0, 1), 6),
        (kr_ref, vr_ref, 0, (0, 1), 8),
        (kr_ref, vr_ref, f, (1,), 10),
        (tk_ref, tv_ref, 0, (0, 1), None),
    )
    inv_rows, delta_rows, q_scaled, g_scaled = [], [], [], []
    for frame in range(2):
        cols = slice(frame * f, (frame + 1) * f)
        query = q_ref[cols, :]
        grad = g_ref[cols, :]
        top = None
        for c, (k_ref, _, row, frames, tile) in enumerate(chunks):
            if frame not in frames:
                continue
            scores = dot(k_ref[row:row + f, :], query, NT)
            s_scr[c * f:(c + 1) * f, cols] = scores
            for t in range(2):
                part = fold_rows(scores[t * TILE:(t + 1) * TILE], jnp.max)
                if tile is not None:
                    part = part - bias_ref[tile + t:tile + t + 1, cols]
                top = part if top is None else jnp.maximum(top, part)
        top = jnp.max(top, axis=0, keepdims=True) * EXP2_SCALE
        total = jnp.zeros((8, f), jnp.float32)
        delta = jnp.zeros((8, f), jnp.float32)
        for c, (_, v_ref, row, frames, tile) in enumerate(chunks):
            if frame not in frames:
                continue
            dprobs = dot(v_ref[row:row + f, :], grad, NT)
            dp_scr[c * f:(c + 1) * f, cols] = dprobs.astype(jnp.bfloat16)
            for t in range(2):
                rows = slice(c * f + t * TILE, c * f + (t + 1) * TILE)
                shift = top
                if tile is not None:
                    shift = shift + bias_ref[tile + t:tile + t + 1, cols]
                weights = jnp.exp2(s_scr[rows, cols] * EXP2_SCALE - shift)
                e_scr[rows, cols] = weights.astype(jnp.bfloat16)
                total = total + fold_rows(weights, jnp.sum)
                delta = delta + fold_rows(weights * dprobs[t * TILE:(t + 1) * TILE], jnp.sum)
        inv = 1.0 / jnp.sum(total, axis=0, keepdims=True)
        delta_rows.append(jnp.sum(delta, axis=0, keepdims=True) * inv)
        inv_rows.append(inv)
        inv_col = jnp.transpose(jnp.broadcast_to(inv, (D_HEAD, f)))
        q_scaled.append((query.astype(jnp.float32) * (inv_col * SCALE)).astype(jnp.bfloat16))
        g_scaled.append((grad.astype(jnp.float32) * inv_col).astype(jnp.bfloat16))
    q_both = jnp.concatenate(q_scaled, axis=0)
    g_both = jnp.concatenate(g_scaled, axis=0)
    delta_both = jnp.concatenate(delta_rows, axis=1)
    inv_both = jnp.concatenate(inv_rows, axis=1)
    dq_parts = [jnp.zeros((D_HEAD, f), jnp.float32) for _ in range(2)]
    sides = {}
    for c, (k_ref, _, row, frames, _) in enumerate(chunks):
        rows = slice(c * f, (c + 1) * f)
        cols = slice(frames[0] * f, (frames[-1] + 1) * f)
        weights = e_scr[rows, cols]
        dscores = (weights.astype(jnp.float32) * (dp_scr[rows, cols].astype(jnp.float32) - delta_both[:, cols])).astype(jnp.bfloat16)
        value_term = dot(weights, g_both[cols], NN)
        key_term = dot(dscores, q_both[cols], NN)
        key = k_ref[row:row + f, :]
        for frame in frames:
            part = slice(frame * f - cols.start, (frame + 1) * f - cols.start)
            dq_parts[frame] = dq_parts[frame] + dot(key, dscores[:, part], TN)
        if k_ref is ko_ref:
            do_ref[row:row + f, :] = key_term.astype(jnp.bfloat16)
            do_ref[tok + row:tok + row + f, :] = value_term.astype(jnp.bfloat16)
        elif k_ref is tk_ref:
            own = txt_own
            pair = jnp.stack([term.reshape(-1, own, D_HEAD) for term in (key_term, value_term)], axis=1)
            dt_ref[...] = pair.reshape(dt_ref.shape).astype(jnp.bfloat16)
        else:
            sides[k_ref is kr_ref, row] = key_term.astype(jnp.bfloat16), value_term.astype(jnp.bfloat16)
            if k_ref is kr_ref:
                for kind in range(2):
                    to_left, to_right = sides[False, row][kind], sides[True, row][kind]
                    rows = slice(kind * tok + row, kind * tok + row + f)
                    da_ref[rows, :] = jnp.where(even, to_right, to_left)
                    db_ref[rows, :] = jnp.where(even, to_left, to_right)
    for frame in range(2):
        cols = slice(frame * f, (frame + 1) * f)
        query_grad = jnp.transpose(dq_parts[frame] * (inv_both[:, cols] * SCALE))
        dq_ref[cols, :] = unrotate(query_grad, cos_ref[cols, :], sin_ref[cols, :]).astype(jnp.bfloat16)


def attend(txt_own, place, bias, cosine, sine, query, grad, key, value, left, right, text, before, first, heads):
    tok, width = query.shape
    txt = text.shape[0]
    all_heads = width // D_HEAD
    wide = heads * D_HEAD
    whole = lambda shape: pl.BlockSpec(shape, lambda h: (0, 0))
    here = pl.BlockSpec((tok, D_HEAD), lambda h: (0, first + h))
    upper = pl.BlockSpec((tok, D_HEAD), lambda h: (0, h))
    lower = pl.BlockSpec((tok, D_HEAD), lambda h: (1, h))
    text_k = pl.BlockSpec((txt, D_HEAD), lambda h: (0, first + h))
    text_v = pl.BlockSpec((txt, D_HEAD), lambda h: (0, all_heads + first + h))
    both = pl.BlockSpec((2 * tok, D_HEAD), lambda h: (0, h))
    in_specs = [pl.BlockSpec(memory_space=pltpu.SMEM), whole(bias.shape), whole(cosine.shape), whole(sine.shape), here, here, here, here,
                upper, lower, upper, lower, text_k, text_v]
    operands = [place, bias, cosine, sine, query, grad, key, value, left, left, right, right, text, text]
    aliases = {}
    if before is not None:
        aliases = {len(operands): 0, len(operands) + 1: 4}
        in_specs += [pl.BlockSpec(memory_space=pl.ANY)] * 2
        operands += list(before)
    keys = 3 * tok + txt
    pairs = tok * (5 * FRAME + txt) * heads
    return pl.pallas_call(
        functools.partial(attend_body, aliased=before is not None, txt_own=txt_own),
        grid=(heads,),
        in_specs=in_specs,
        out_specs=[here, both, both, both, pl.BlockSpec((2 * txt, D_HEAD), lambda h: (0, first + h))],
        out_shape=[
            jax.ShapeDtypeStruct((tok, width), jnp.bfloat16),
            jax.ShapeDtypeStruct((2 * tok, wide), jnp.bfloat16),
            jax.ShapeDtypeStruct((2 * tok, wide), jnp.bfloat16),
            jax.ShapeDtypeStruct((2 * tok, wide), jnp.bfloat16),
            jax.ShapeDtypeStruct((2 * txt, width), jnp.bfloat16),
        ],
        scratch_shapes=[
            pltpu.VMEM((keys, tok), jnp.float32),
            pltpu.VMEM((keys, tok), jnp.bfloat16),
            pltpu.VMEM((keys, tok), jnp.bfloat16),
        ] + [pltpu.VMEM((tok, D_HEAD), jnp.bfloat16)] * 4,
        input_output_aliases=aliases,
        compiler_params=pltpu.CompilerParams(vmem_limit_bytes=60 * 2**20),
        cost_estimate=pl.CostEstimate(flops=pairs, bytes_accessed=tok * wide, transcendentals=0),
        name="attend",
    )(*operands)


def finish_body(*refs, aliased):
    cos_ref, sin_ref, ok_ref, ov_ref, ak_ref, av_ref, bk_ref, bv_ref = refs[:8]
    key_ref, value_ref = refs[8 + (2 if aliased else 0):]
    up = lambda ref, cols: ref[:, cols].astype(jnp.float32)
    cosine, sine = cos_ref[...], sin_ref[...]
    for head in range(ok_ref.shape[1] // D_HEAD):
        cols = slice(head * D_HEAD, (head + 1) * D_HEAD)
        key_grad = up(ok_ref, cols) + up(ak_ref, cols) + up(bk_ref, cols)
        key_ref[:, cols] = unrotate(key_grad, cosine, sine).astype(jnp.bfloat16)
        value_ref[:, cols] = (up(ov_ref, cols) + up(av_ref, cols) + up(bv_ref, cols)).astype(jnp.bfloat16)


def finish(cosine, sine, own, back_a, back_b, before, first, width):
    tok, wide = own.shape[0] // 2, own.shape[1]
    step = tok // 2
    upper = pl.BlockSpec((step, wide), lambda r: (r, 0))
    lower = pl.BlockSpec((step, wide), lambda r: (tok // step + r, 0))
    table = pl.BlockSpec((step, D_HEAD), lambda r: (r, 0))
    here = pl.BlockSpec((step, wide), lambda r: (r, first * D_HEAD // wide))
    in_specs = [table, table] + [upper, lower] * 3
    operands = [cosine, sine, own, own, back_a, back_a, back_b, back_b]
    aliases = {}
    if before is not None:
        in_specs += [pl.BlockSpec(memory_space=pl.ANY)] * 2
        operands += list(before)
        aliases = {8: 0, 9: 1}
    return pl.pallas_call(
        functools.partial(finish_body, aliased=before is not None),
        grid=(tok // step,),
        in_specs=in_specs,
        out_specs=[here, here],
        out_shape=[jax.ShapeDtypeStruct((tok, width), jnp.bfloat16)] * 2,
        input_output_aliases=aliases,
        compiler_params=pltpu.CompilerParams(vmem_limit_bytes=16 * 2**20),
        cost_estimate=pl.CostEstimate(flops=10 * tok * wide, bytes_accessed=20 * tok * wide, transcendentals=0),
        name="finish",
    )(*operands)


def shards(query_rot, key_rot, value, grad_out, text_key, text_value, positions, tile_mask):
    tok, width = query_rot.shape
    head_count = width // D_HEAD
    sizes = [head_count * share // sum(SPLIT) for share in SPLIT]
    firsts = [sum(sizes[:group]) for group in range(len(sizes))]
    tiles = tok // TILE
    ctx_size = lax.axis_size("ctx")
    ctx_index = lax.axis_index("ctx")
    text_own = jnp.concatenate([text_key, text_value], axis=1)
    near, far = text_groups(ctx_size)

    def packed(keys, values, group):
        cols = slice(firsts[group] * D_HEAD, (firsts[group] + sizes[group]) * D_HEAD)
        return jnp.concatenate([keys[:, cols], values[:, cols]], axis=0)

    pair = packed(key_rot, value, 0)
    halos = [(exchange(pair, "ctx", 0), exchange(pair, "ctx", 1))]
    text = lax.all_to_all(jnp.tile(text_own, (ctx_size, 1)), "ctx", 0, 0, tiled=True)
    padded = jnp.pad(tile_mask, ((0, 0), (tiles, tiles)))
    block = lax.dynamic_slice(padded, (ctx_index * tiles, ctx_index * tiles), (tiles, 3 * tiles))
    bias = jnp.where(jnp.repeat(block.T > 0, TILE, axis=1), 0.0, BLOCKED).astype(jnp.float32)
    tables = rope_tables(positions)
    near_pair, keys_later, values_later = lax.optimization_barrier((halos[0][0], key_rot, value))
    pairs = [packed(keys_later, values_later, group) for group in range(1, len(sizes))]
    first_halves = [exchange(pair, "ctx", 0) for pair in pairs]
    far_pair, (cosine, sine), bias, pairs = lax.optimization_barrier((halos[0][1], tables, bias, pairs))
    halos = [(near_pair, far_pair)] + [(half, exchange(pair, "ctx", 1)) for half, pair in zip(first_halves, pairs)]
    place = jnp.full((1,), ctx_index, jnp.int32)
    before, waiting, done = None, None, None
    for group, (first, heads) in enumerate(zip(firsts, sizes)):
        query_grad, own, to_even, to_odd, text_part = attend(
            text_key.shape[0], place, bias, cosine, sine, query_rot, grad_out, key_rot, value, *halos[group], text,
            before, first, heads)
        if waiting is not None:
            done = finish(cosine, sine, *waiting, done, firsts[group - 1], width)
        before = query_grad, text_part
        waiting = (own, exchange(to_even, "ctx", 0), exchange(to_odd, "ctx", 1))
    done = finish(cosine, sine, *waiting, done, firsts[-1], width)

    def reduce_text(rows):
        return part_sum(lax.all_to_all(rows, "ctx", 0, 0, tiled=True), ctx_size)

    own = text_key.shape[0]
    passes = jnp.minimum(tile_mask[0, 0] + 1, 1)
    text_grads = lax.fori_loop(
        0, passes, lambda step, _: reduce_text(lax.optimization_barrier((text_part, step))[0]), jnp.concatenate([text_key, text_value], axis=0))
    return query_grad, done[0], done[1], text_grads[:own], text_grads[own:]


def solution(mesh):
    spread = P("ctx", "tp")
    return jax.shard_map(
        shards,
        mesh=mesh,
        in_specs=(spread,) * 6 + (P(None, "ctx"), P()),
        out_specs=(spread,) * 5,
        check_vma=False,
    )
```
